32 devices in a mesh: gx: 4 (over z), gy: 8 (over y, x, core).
Axes of the slice: x: 2, y: 2, z: 4, core: 2. Of those that a mesh axis runs over, the one named last changes fastest.
Arguments:
- tokens: bfloat16 [8192, 1664], P('gy', 'gx'), may hold values from -6 to 6
- segment_ids: int32 [8192], P('gy'), may hold values from 0 to 255, as said below
- first_gain: float32 [1664], replicated, may hold values from 0.5 to 2
- first_bias: float32 [1664], replicated, may hold values from -3 to 3
- query_key_value: bfloat16 [3, 1664, 1664], P(None, 'gy', 'gx'), may hold values from -0.15625 to 0.15625
- project_out: bfloat16 [1664, 1664], P('gx', 'gy'), may hold values from -0.15625 to 0.15625
- second_gain: float32 [1664], replicated, may hold values from 0.5 to 2
- second_bias: float32 [1664], replicated, may hold values from -3 to 3
- up_weight: bfloat16 [1664, 8192], P('gy', 'gx'), may hold values from -0.15625 to 0.15625
- down_weight: bfloat16 [8192, 1664], P('gx', 'gy'), may hold values from -0.0625 to 0.0625
- final_gain: float32 [1664], replicated, may hold values from 0.5 to 2
- final_bias: float32 [1664], replicated, may hold values from -3 to 3
- merge_weight: bfloat16 [4, 1664, 1664], P(None, 'gx', 'gy'), may hold values from -0.078125 to 0.078125
- owners: int32 [2048, 1], P('gy'), may hold values from 0 to 7; in each aligned block of 256 rows (0 to 255, 256 to 511, ...) at most 64 rows name the same one
Outputs:
- delivered: bfloat16 [8, 8, 64, 1664], P('gy', None, None, 'gx')
The draws below stay inside these ranges and needn't reach their ends.
Inputs may be any that keep to these rules, and one draw needn't show every extreme that they name: `segment_ids`: each segment is a run of whole units of 32 consecutive tokens that lies inside one aligned block of 1024 tokens; ids never fall along the tokens and differ between segments. `owners`: in each aligned block of 256 rows (the merged tokens of one index of gy), no owner is named by more than 64 rows.
All inputs are finite; a program needn't handle non-finite values.
Results may differ from the reference program's by a relative error of at most 0.02.
Values may be sent and summed in bfloat16 or wider, within the bound.
A program may use at most 128 MiB of HBM per device.

```python
import math
import jax
import jax.numpy as jnp
import numpy as np
from jax import lax

D = 1664
HEADS = 16
HEAD = 104
FF = 8192
IMG_W = 16
TOK_DEV = 1024
TOKENS = 8192
MERGED_DEV = 256
MERGED = 2048
CAP = 64
N_GY = 8


def draw_segment_ids(key, part):
    unit_count = TOKENS // (2 * IMG_W)
    per_block = TOK_DEV // (2 * IMG_W)
    coin = jax.random.randint(key, (unit_count,), 0, 3)
    unit_index = jnp.arange(unit_count, dtype=jnp.int32)
    forced = (unit_index % per_block == 0) | (unit_index == unit_count - 1)
    starts = forced | (coin == 0)
    first_unit = lax.cummax(jnp.where(starts, unit_index, 0).astype(jnp.int32), axis=0)
    return jnp.repeat(first_unit, 2 * IMG_W).astype(jnp.int32)


def level_of(own_key, extent, cuts, least, largest):
    level, own = 1.0, jax.random.fold_in(own_key, 6)
    for position, parts in cuts:
        heights = jnp.exp(jax.random.uniform(jax.random.fold_in(own, position), (parts,), jnp.float32, least / len(cuts), largest / len(cuts)))
        level = level * jnp.repeat(heights, extent[position] // parts).reshape([-1 if axis == position else 1 for axis in range(len(extent))])
    return level


def deal_out(key, own, number, rows, number_of, top, limit, slope):
    ranking = jax.random.permutation(key, number_of)
    heavy_load, ordinary = portions_of(number_of, rows * top, limit, slope, True), portions_of(number_of, rows * top, limit, slope, False)
    places = jnp.arange(number_of)

    def named(sizes, turn):
        used = int((sizes > 0).sum())
        fixed = max(1, used // 4)
        passed = fixed + (places - fixed + turn * (used - fixed)) % max(1, number_of - fixed)
        return jnp.zeros((number_of,), jnp.int32).at[ranking[jnp.where(places < fixed, places, passed)]].set(jnp.asarray(sizes, jnp.int32))

    sizes = jnp.where(number % 4 == 0, named(heavy_load, number // 4), named(ordinary, number - number // 4 - 1))
    mixed = jax.random.permutation(jax.random.fold_in(own, 3), number_of)
    source_of, sink = mixed[0:number_of // 2 * 2:2], mixed[1:number_of // 2 * 2:2]
    slack = jnp.minimum(sizes[source_of] - 1, limit - sizes[sink]) // 2
    slack = jnp.where((source_of == ranking[0]) | (sink == ranking[0]) | (sizes[sink] == 0), 0, jnp.maximum(slack, 0))
    passed = jax.random.randint(jax.random.fold_in(own, 4), (number_of // 2,), 0, 1 << 20) % (slack + 1)
    sizes = sizes.at[source_of].add(-passed).at[sink].add(passed)
    items = jnp.searchsorted(jnp.cumsum(sizes), jnp.arange(rows * top), side="right").astype(jnp.int32)
    table = items.reshape(top, rows).T
    table = table[jax.random.permutation(jax.random.fold_in(own, 1), rows)]
    turn = jax.random.randint(jax.random.fold_in(own, 2), (rows, 1), 0, top)
    return jnp.take_along_axis(table, (jnp.arange(top)[None, :] + turn) % top, axis=1)


def portions_of(amount, total, bound, lean, full):
    loads = [(1 << 20) // math.isqrt(grade ** lean) + 1 for grade in range(1, amount + 1)]
    largest = bound if full else min(bound, max(-(-total // amount), total * loads[0] // sum(loads)))
    least = 1 if total - largest >= amount - 1 else 0
    given, spare = [largest] + [least] * (amount - 1), total - largest - least * (amount - 1)
    while spare > 0:
        movable = [i for i in range(1, amount) if given[i] < largest] or [i for i in range(1, amount) if given[i] < bound]
        whole, remaining = sum([loads[i] for i in movable]), spare
        for i in movable:
            extra = min(bound - given[i], max(1, remaining * loads[i] // whole), spare)
            given[i] = given[i] + extra
            spare = spare - extra
    return np.array(given)


def scatter_about(rng, dims, scale, bound, split=(), held_as=jnp.bfloat16):
    values = scale * jax.random.normal(rng, dims, jnp.float32)
    if split:
        values = values * level_of(rng, dims, split, -0.22, 0.18)
    return jnp.clip(values, -bound, bound).astype(held_as)


def setup_inputs(seed: int = 0) -> dict:
    splits = jax.random.split(jax.random.key(seed), 15)
    tokens = scatter_about(splits[0], (TOKENS, D), 1.0, 6.0, ((0, 8), (1, 4)))
    segment_ids = draw_segment_ids(jax.random.fold_in(splits[14], 71), 0)
    first_gain = jnp.clip(jnp.exp(jax.random.uniform(splits[2], (D,), jnp.float32, math.log(0.5), math.log(2.0))), 0.5, 2.0)
    first_bias = scatter_about(splits[3], (D,), 0.5, 3.0, (), jnp.float32)
    query_key_value = scatter_about(splits[4], (3, D, D), D ** -0.5, 0.15625, ((1, 8), (2, 4)))
    project_out = scatter_about(splits[5], (D, D), D ** -0.5, 0.15625, ((0, 4), (1, 8)))
    second_gain = jnp.clip(jnp.exp(jax.random.uniform(splits[6], (D,), jnp.float32, math.log(0.5), math.log(2.0))), 0.5, 2.0)
    second_bias = scatter_about(splits[7], (D,), 0.5, 3.0, (), jnp.float32)
    up_weight = scatter_about(splits[8], (D, FF), D ** -0.5, 0.15625, ((0, 8), (1, 4)))
    down_weight = scatter_about(splits[9], (FF, D), FF ** -0.5, 0.0625, ((0, 4), (1, 8)))
    final_gain = jnp.clip(jnp.exp(jax.random.uniform(splits[10], (D,), jnp.float32, math.log(0.5), math.log(2.0))), 0.5, 2.0)
    final_bias = scatter_about(splits[11], (D,), 0.5, 3.0, (), jnp.float32)
    merge_weight = scatter_about(splits[12], (4, D, D), (4 * D) ** -0.5, 0.078125, ((1, 4), (2, 8)))
    owners_keys = jax.random.split(jax.random.fold_in(splits[13], 1), MERGED // MERGED_DEV)
    owners_turns = jax.random.permutation(jax.random.fold_in(splits[13], 3), MERGED // MERGED_DEV)
    owners = jax.vmap(lambda own, number: deal_out(jax.random.fold_in(splits[13], 2), own, number, MERGED_DEV, N_GY, 1, CAP, 2))(owners_keys, owners_turns).reshape((MERGED, 1))
    return {"tokens": tokens, "segment_ids": segment_ids, "first_gain": first_gain, "first_bias": first_bias, "query_key_value": query_key_value, "project_out": project_out, "second_gain": second_gain, "second_bias": second_bias, "up_weight": up_weight, "down_weight": down_weight, "final_gain": final_gain, "final_bias": final_bias, "merge_weight": merge_weight, "owners": owners}


EPSILON = 1e-06

def layer_norm(values, gain, bias):
    values = values.astype(jnp.float32)
    center = values - lax.optimization_barrier(jnp.mean(values, axis=-1, keepdims=True))
    spread = lax.optimization_barrier(jnp.mean(center * center, axis=-1, keepdims=True))
    return center * lax.rsqrt(spread + EPSILON) * gain + bias

def attend(query_rows, key_rows, value_rows, query_ids, key_ids):
    scores = jnp.einsum('qhe,khe->hqk', query_rows.astype(jnp.float32), key_rows.astype(jnp.float32)) * HEAD ** (-0.5)
    same_segment = query_ids[None, :, None] == key_ids[None, None, :]
    scores = jnp.where(same_segment, scores, -1e+30)
    highest = lax.optimization_barrier(jnp.max(scores, axis=-1, keepdims=True))
    raised = jnp.exp(scores - highest)
    shares = (raised / lax.optimization_barrier(jnp.sum(raised, axis=-1, keepdims=True))).astype(jnp.bfloat16)
    return jnp.einsum('hqk,khe->qhe', shares.astype(jnp.float32), value_rows.astype(jnp.float32)).astype(jnp.bfloat16)

def reference(tokens, segment_ids, first_gain, first_bias, query_key_value, project_out, second_gain, second_bias, up_weight, down_weight, final_gain, final_bias, merge_weight, owners):
    normed = layer_norm(tokens, first_gain, first_bias).astype(jnp.bfloat16)
    qkv = jnp.einsum('td,kdc->ktc', normed.astype(jnp.float32), query_key_value.astype(jnp.float32)).astype(jnp.bfloat16)
    queries = qkv[0].reshape(TOKENS, HEADS, HEAD)
    key_all = qkv[1].reshape(TOKENS, HEADS, HEAD)
    value_all = qkv[2].reshape(TOKENS, HEADS, HEAD)
    query_block = min(512, TOK_DEV)

    def one_block(index):
        first_query = index * query_block
        first_key = first_query // TOK_DEV * TOK_DEV
        query_rows = lax.dynamic_slice_in_dim(queries, first_query, query_block, 0)
        key_rows = lax.dynamic_slice_in_dim(key_all, first_key, TOK_DEV, 0)
        value_rows = lax.dynamic_slice_in_dim(value_all, first_key, TOK_DEV, 0)
        query_ids = lax.dynamic_slice_in_dim(segment_ids, first_query, query_block, 0)
        key_ids = lax.dynamic_slice_in_dim(segment_ids, first_key, TOK_DEV, 0)
        return attend(query_rows, key_rows, value_rows, query_ids, key_ids)
    attended = lax.map(one_block, jnp.arange(TOKENS // query_block, dtype=jnp.int32)).reshape(TOKENS, D)
    first_resid = (tokens.astype(jnp.float32) + jnp.dot(attended, project_out, preferred_element_type=jnp.float32)).astype(jnp.bfloat16)
    second_normed = layer_norm(first_resid, second_gain, second_bias).astype(jnp.bfloat16)
    upper = jnp.dot(second_normed, up_weight, preferred_element_type=jnp.float32)
    hidden = jax.nn.gelu(upper, approximate=False).astype(jnp.bfloat16)
    second_resid = (first_resid.astype(jnp.float32) + jnp.dot(hidden, down_weight, preferred_element_type=jnp.float32)).astype(jnp.bfloat16)
    final_normed = layer_norm(second_resid, final_gain, final_bias).astype(jnp.bfloat16)
    grouped = final_normed.reshape(TOKENS // (2 * IMG_W), 2, IMG_W // 2, 2, D).transpose(0, 2, 1, 3, 4).reshape(MERGED, 4, D)
    projected = jnp.einsum('pkf,kfc->pc', grouped.astype(jnp.float32), merge_weight.astype(jnp.float32)).astype(jnp.bfloat16)
    owner_col = owners[:, 0].astype(jnp.int32)
    one_hot = (owner_col[:, None] == jnp.arange(N_GY, dtype=jnp.int32)[None, :]).astype(jnp.int32)
    one_hot = one_hot.reshape(N_GY, MERGED_DEV, N_GY)
    slot_rank = lax.optimization_barrier(jnp.sum((jnp.cumsum(one_hot, axis=1) - 1) * one_hot, axis=-1)).reshape(MERGED).astype(jnp.int32)
    source_idx = (jnp.arange(MERGED, dtype=jnp.int32) // MERGED_DEV).astype(jnp.int32)
    delivered = jnp.zeros((N_GY, N_GY, CAP, D), jnp.bfloat16).at[owner_col, source_idx, slot_rank].set(projected)
    return delivered
```

```python
import jax
import jax.numpy as jnp
from jax import lax
from jax.sharding import PartitionSpec as P

HEAD = 104
IMG_W = 16
FIRST_CHUNKS = 2
MAIN_CHUNKS = 4


EPSILON = 1e-06


def normalize_rows(values, gain, bias):
    values = values.astype(jnp.float32)
    center = values - jnp.mean(values, axis=-1, keepdims=True)
    spread = jnp.mean(center * center, axis=-1, keepdims=True)
    return center * lax.rsqrt(spread + EPSILON) * gain + bias


def normalize_from_sums(values, sums, features, gain, bias):
    values = values.astype(jnp.float32)
    row_mean = sums[0] / features
    spread = sums[1] / features - row_mean * row_mean
    return (values - row_mean[:, None]) * lax.rsqrt(spread[:, None] + EPSILON) * gain + bias


def own_slice(vector, width):
    return lax.dynamic_slice_in_dim(vector, lax.axis_index("gx") * width, width, 0)


def row_sums(values):
    values = values.astype(jnp.float32)
    return jnp.stack([jnp.sum(values, axis=-1), jnp.sum(values * values, axis=-1)])


def line_gather(own):
    count = lax.axis_size("gx")
    place = lax.axis_index("gx")
    from_left, from_right = [own], [own]
    for step in range(1, count):
        up_pairs = [(i, i + 1) for i in range(step - 1, count - 1)]
        down_pairs = [(i, i - 1) for i in range(1, count - step + 1)]
        from_left.append(lax.ppermute(from_left[-1], "gx", up_pairs))
        from_right.append(lax.ppermute(from_right[-1], "gx", down_pairs))
    blocks = []
    for j in range(count):
        block = from_left[0]
        for i in range(count):
            if i != j:
                other = from_left[i - j] if i > j else from_right[j - i]
                block = jnp.where(place == i, other, block)
        blocks.append(block)
    return blocks


def line_scatter(term):
    count = lax.axis_size("gx")
    terms = {}

    def part(s):
        if s not in terms:
            terms[s] = term(s)
        return terms[s]

    rightward = leftward = None
    for step in range(1, count):
        up_sum = part(count - step)
        down_sum = part(step)
        if rightward is not None:
            up_sum = up_sum + rightward.astype(jnp.float32)
            down_sum = down_sum + leftward.astype(jnp.float32)
        rightward = lax.ppermute(
            up_sum.astype(jnp.bfloat16), "gx", [(i, i + 1) for i in range(step)]
        )
        leftward = lax.ppermute(
            down_sum.astype(jnp.bfloat16),
            "gx",
            [(i, i - 1) for i in range(count - step, count)],
        )
    total = part(0)
    if rightward is not None:
        total = total + rightward.astype(jnp.float32) + leftward.astype(jnp.float32)
    return total


def rows_for(weight_rows, s, width):
    count = lax.axis_size("gx")
    dest = lax.rem(lax.axis_index("gx") + s, count)
    return lax.dynamic_slice_in_dim(weight_rows, dest * width, width, 0)


def dot_rows(left, right):
    return lax.dot_general(
        left, right, (((1,), (1,)), ((), ())), preferred_element_type=jnp.float32
    )


def attend(queries, query_ids, key_rows, value_rows, segment_ids):
    scores = jnp.einsum(
        "qhe,khe->hqk", queries, key_rows, preferred_element_type=jnp.float32
    ) * HEAD ** (-0.5)
    same_segment = query_ids[None, :, None] == segment_ids[None, None, :]
    scores = jnp.where(same_segment, scores, -1e30)
    highest = jnp.max(scores, axis=-1, keepdims=True)
    raised = jnp.exp(scores - highest)
    total = jnp.sum(raised, axis=-1)
    mixed = jnp.einsum(
        "hqk,khe->qhe",
        raised.astype(jnp.bfloat16),
        value_rows,
        preferred_element_type=jnp.float32,
    )
    mixed = (mixed / total.T[:, :, None]).astype(jnp.bfloat16)
    return mixed.reshape(mixed.shape[0], -1)


def row_chunks(rows, wanted):
    unit = 2 * IMG_W
    count = wanted
    while count > 1 and rows % (count * unit):
        count //= 2
    return count, rows // count


def body(
    tokens,
    segment_ids,
    first_gain,
    first_bias,
    query_key_value,
    project_out,
    second_gain,
    second_bias,
    up_weight,
    down_weight,
    final_gain,
    final_bias,
    merge_weight,
    owners,
):
    tok_rows = tokens.shape[0]
    width = tokens.shape[1]
    features = width * lax.axis_size("gx")
    qkv_full = lax.all_gather(query_key_value, "gy", axis=1, tiled=True)
    out_rows = lax.all_gather(project_out.T, "gy", axis=0, tiled=True)
    up_full = lax.all_gather(up_weight, "gy", axis=0, tiled=True)
    down_rows = lax.all_gather(down_weight.T, "gy", axis=0, tiled=True)
    merge_rows = lax.all_gather(
        merge_weight.transpose(2, 0, 1).reshape(merge_weight.shape[2], 4 * width),
        "gy",
        axis=0,
        tiled=True,
    )

    count, size = row_chunks(tok_rows, FIRST_CHUNKS)
    qkv_parts = []
    for c in range(count):
        own = tokens[c * size : (c + 1) * size]
        full_rows = jnp.concatenate(line_gather(own), axis=1)
        normed = normalize_rows(full_rows, first_gain, first_bias).astype(jnp.bfloat16)
        qkv_parts.append(
            jnp.einsum(
                "td,kdc->ktc", normed, qkv_full, preferred_element_type=jnp.float32
            ).astype(jnp.bfloat16)
        )
    qkv = jnp.concatenate(qkv_parts, axis=1)
    head_count = qkv.shape[2] // HEAD
    queries = qkv[0].reshape(tok_rows, head_count, HEAD)
    key_rows = qkv[1].reshape(tok_rows, head_count, HEAD)
    value_rows = qkv[2].reshape(tok_rows, head_count, HEAD)

    count, size = row_chunks(tok_rows, MAIN_CHUNKS)
    projected_parts = []
    own_final_gain = own_slice(final_gain, width)
    own_final_bias = own_slice(final_bias, width)
    for c in range(count):
        rows = slice(c * size, (c + 1) * size)
        attended = attend(queries[rows], segment_ids[rows], key_rows, value_rows, segment_ids)
        attn_share = line_scatter(lambda s: dot_rows(attended, rows_for(out_rows, s, width)))
        first_resid = (tokens[rows].astype(jnp.float32) + attn_share).astype(jnp.bfloat16)
        resid_rows = jnp.concatenate(line_gather(first_resid), axis=1)
        second_normed = normalize_rows(resid_rows, second_gain, second_bias).astype(
            jnp.bfloat16
        )
        upper = jnp.dot(second_normed, up_full, preferred_element_type=jnp.float32)
        hidden = jax.nn.gelu(upper, approximate=False).astype(jnp.bfloat16)
        mlp_share = line_scatter(lambda s: dot_rows(hidden, rows_for(down_rows, s, width)))
        second_resid = (first_resid.astype(jnp.float32) + mlp_share).astype(jnp.bfloat16)
        post_sums = sum(line_gather(row_sums(second_resid)))
        final_normed = normalize_from_sums(
            second_resid, post_sums, features, own_final_gain, own_final_bias
        ).astype(jnp.bfloat16)
        grouped = (
            final_normed.reshape(size // (2 * IMG_W), 2, IMG_W // 2, 2, width)
            .transpose(0, 2, 1, 3, 4)
            .reshape(size // 4, 4 * width)
        )
        projected_parts.append(
            line_scatter(lambda s: dot_rows(grouped, rows_for(merge_rows, s, width))).astype(
                jnp.bfloat16
            )
        )
    projected = jnp.concatenate(projected_parts, axis=0)

    merged_rows = tok_rows // 4
    owner_count = lax.axis_size("gy")
    capacity = max(2, 2 * merged_rows // owner_count)
    owner_col = owners[:, 0]
    order = jnp.arange(merged_rows, dtype=jnp.int32)
    earlier = (owner_col[:, None] == owner_col[None, :]) & (order[None, :] < order[:, None])
    slot_rank = jnp.sum(earlier.astype(jnp.int32), axis=1)
    target = owner_col * capacity + slot_rank
    place = (
        jnp.arange(owner_count * capacity, dtype=jnp.int32)[:, None] == target[None, :]
    ).astype(jnp.bfloat16)
    outgoing = jnp.dot(place, projected, preferred_element_type=jnp.float32).astype(jnp.bfloat16)
    outgoing = outgoing.reshape(owner_count, capacity, width)
    arrived = lax.all_to_all(outgoing, "gy", split_axis=0, concat_axis=0, tiled=True)
    return arrived.reshape(1, owner_count, capacity, width)


def solution(mesh):
    in_specs = (
        P("gy", "gx"),
        P("gy"),
        P(),
        P(),
        P(None, "gy", "gx"),
        P("gx", "gy"),
        P(),
        P(),
        P("gy", "gx"),
        P("gx", "gy"),
        P(),
        P(),
        P(None, "gx", "gy"),
        P("gy", None),
    )
    out_specs = P("gy", None, None, "gx")
    return jax.shard_map(body, mesh=mesh, in_specs=in_specs, out_specs=out_specs, check_vma=False)
```

```python
import functools

import jax
import jax.numpy as jnp
from jax import lax
from jax.experimental import pallas as pl
from jax.experimental.pallas import tpu as pltpu
from jax.sharding import PartitionSpec as P

HEAD = 104
IMG_W = 16
CHUNKS = 4
MESH = pl.DeviceIdType.MESH


EPSILON = 1e-06


def normalize_rows(values, gain, bias):
    values = values.astype(jnp.float32)
    center = values - jnp.mean(values, axis=-1, keepdims=True)
    spread = jnp.mean(center * center, axis=-1, keepdims=True)
    return center * lax.rsqrt(spread + EPSILON) * gain + bias


def normalize_from_sums(values, sums, features, gain, bias):
    values = values.astype(jnp.float32)
    row_mean = sums[0] / features
    spread = sums[1] / features - row_mean * row_mean
    return (values - row_mean[:, None]) * lax.rsqrt(spread[:, None] + EPSILON) * gain + bias


def own_slice(vector, width):
    return lax.dynamic_slice_in_dim(vector, lax.axis_index("gx") * width, width, 0)


def row_sums(values):
    values = values.astype(jnp.float32)
    return jnp.stack([jnp.sum(values, axis=-1), jnp.sum(values * values, axis=-1)])


def line_kernel(count, chunks, size, scatter, gather, has_base, *refs):
    refs = list(refs)
    terms = [refs.pop(0) for _ in range(count)] if scatter else None
    base = refs.pop(0) if has_base else None
    out = refs.pop(0)
    if scatter:
        inbox, scatter_sends, scatter_recvs = refs[0], refs[1], refs[2]
        refs = refs[3:]
    if gather:
        gather_sends, gather_recvs = refs[0], refs[1]
    me = lax.axis_index("gx")
    has_left, has_right = me > 0, me < count - 1
    barrier = pltpu.get_barrier_semaphore()

    @pl.when(has_left)
    def _():
        pl.semaphore_signal(barrier, inc=1, device_id={"gx": me - 1}, device_id_type=MESH)

    @pl.when(has_right)
    def _():
        pl.semaphore_signal(barrier, inc=1, device_id={"gx": me + 1}, device_id_type=MESH)

    @pl.when(has_left & has_right)
    def _():
        pl.semaphore_wait(barrier, 2)

    @pl.when(jnp.logical_not(has_left & has_right))
    def _():
        pl.semaphore_wait(barrier, 1)

    def target(way):
        return {"gx": me + 1 - 2 * way}

    def rows(c):
        return pl.ds(c * size, size)

    def scatter_copy(way, c, d, src):
        return pltpu.make_async_remote_copy(
            src_ref=src,
            dst_ref=inbox.at[way, c, d],
            send_sem=scatter_sends.at[way, c, d],
            recv_sem=scatter_recvs.at[way, c, d],
            device_id=target(way),
            device_id_type=MESH,
        )

    def gather_copy(way, c, j):
        block = out.at[j, rows(c)]
        return pltpu.make_async_remote_copy(
            src_ref=block,
            dst_ref=block,
            send_sem=gather_sends.at[way, c, j],
            recv_sem=gather_recvs.at[way, c, j],
            device_id=target(way),
            device_id_type=MESH,
        )

    def beyond(way, d):
        return me < d if way == 0 else me > d

    def pass_on(c):
        for k in range(count - 1):
            for way in (0, 1):
                d = count - 1 - k if way == 0 else k
                first = me == 0 if way == 0 else me == count - 1

                @pl.when(beyond(way, d) & first)
                def _():
                    scatter_copy(way, c, d, terms[d].at[rows(c)]).start()

                @pl.when(beyond(way, d) & jnp.logical_not(first))
                def _():
                    scatter_copy(way, c, d, inbox.at[way, c, d]).wait_recv()
                    total = inbox[way, c, d].astype(jnp.float32) + terms[d][rows(c)].astype(
                        jnp.float32
                    )
                    inbox[way, c, d] = total.astype(jnp.bfloat16)
                    scatter_copy(way, c, d, inbox.at[way, c, d]).start()

    def settle(c):
        if scatter:
            for d in range(count):

                @pl.when(me == d)
                def _():
                    total = terms[d][rows(c)].astype(jnp.float32)
                    if has_base:
                        total = total + base[rows(c)].astype(jnp.float32)
                    if d > 0:
                        scatter_copy(0, c, d, inbox.at[0, c, d]).wait_recv()
                        total = total + inbox[0, c, d].astype(jnp.float32)
                    if d < count - 1:
                        scatter_copy(1, c, d, inbox.at[1, c, d]).wait_recv()
                        total = total + inbox[1, c, d].astype(jnp.float32)
                    if gather:
                        out[d, rows(c)] = total.astype(jnp.bfloat16)
                    else:
                        out[rows(c)] = total.astype(jnp.bfloat16)
        else:
            out[me, rows(c)] = base[rows(c)]
        if gather:
            for way in (0, 1):

                @pl.when(has_right if way == 0 else has_left)
                def _():
                    gather_copy(way, c, me).start()

    def forward(c, step):
        for way in (0, 1):
            j = me - step if way == 0 else me + step
            held = j >= 0 if way == 0 else j < count

            @pl.when(held)
            def _():
                gather_copy(way, c, j).wait_recv()

                @pl.when(has_right if way == 0 else has_left)
                def _():
                    gather_copy(way, c, j).start()

    lead = 1 if scatter else 0
    for turn in range(chunks + lead + count - 1):
        if scatter and turn < chunks:
            pass_on(turn)
        if 0 <= turn - lead < chunks:
            settle(turn - lead)
        if gather:
            for step in range(1, count):
                if 0 <= turn - lead - step < chunks:
                    forward(turn - lead - step, step)
    for c in range(chunks):
        for way in (0, 1):
            for d in range(count):
                if scatter:

                    @pl.when(beyond(way, d))
                    def _():
                        scatter_copy(way, c, d, inbox.at[way, c, d]).wait_send()

                if gather:
                    sent = (me >= d) & has_right if way == 0 else (me <= d) & has_left

                    @pl.when(sent)
                    def _():
                        gather_copy(way, c, d).wait_send()


def line_call(terms, base, gather, chunks, collective_id):
    count = lax.axis_size("gx")
    scatter = terms is not None
    some = base if base is not None else terms[0]
    rows, width = some.shape
    while rows % (chunks * 16):
        chunks //= 2
    size = rows // chunks
    scratch = []
    if scatter:
        scratch += [
            pltpu.VMEM((2, chunks, count, size, width), jnp.bfloat16),
            pltpu.SemaphoreType.DMA((2, chunks, count)),
            pltpu.SemaphoreType.DMA((2, chunks, count)),
        ]
    if gather:
        scratch += [
            pltpu.SemaphoreType.DMA((2, chunks, count)),
            pltpu.SemaphoreType.DMA((2, chunks, count)),
        ]
    operands = (list(terms) if scatter else []) + ([base] if base is not None else [])
    shape = (count, rows, width) if gather else (rows, width)
    return pl.pallas_call(
        functools.partial(
            line_kernel, count, chunks, size, scatter, gather, base is not None
        ),
        out_shape=jax.ShapeDtypeStruct(shape, jnp.bfloat16),
        in_specs=[pl.BlockSpec(memory_space=pltpu.VMEM)] * len(operands),
        out_specs=pl.BlockSpec(memory_space=pltpu.VMEM),
        scratch_shapes=scratch,
        compiler_params=pltpu.CompilerParams(
            collective_id=collective_id, has_side_effects=True, vmem_limit_bytes=40 * 2**20
        ),
    )(*operands)


def side_by_side(blocks):
    return jnp.concatenate([blocks[j] for j in range(blocks.shape[0])], axis=1)


def dest_terms(left, weight_rows, width):
    return [
        dot_rows(left, weight_rows[d * width : (d + 1) * width]).astype(jnp.bfloat16)
        for d in range(weight_rows.shape[0] // width)
    ]


def dot_rows(left, right):
    return lax.dot_general(
        left, right, (((1,), (1,)), ((), ())), preferred_element_type=jnp.float32
    )


def attend(queries, query_ids, key_rows, value_rows, segment_ids):
    scores = jnp.einsum(
        "qhe,khe->hqk", queries, key_rows, preferred_element_type=jnp.float32
    ) * HEAD ** (-0.5)
    same_segment = query_ids[None, :, None] == segment_ids[None, None, :]
    scores = jnp.where(same_segment, scores, -1e30)
    highest = jnp.max(scores, axis=-1, keepdims=True)
    raised = jnp.exp(scores - highest)
    total = jnp.sum(raised, axis=-1)
    mixed = jnp.einsum(
        "hqk,khe->qhe",
        raised.astype(jnp.bfloat16),
        value_rows,
        preferred_element_type=jnp.float32,
    )
    mixed = (mixed / total.T[:, :, None]).astype(jnp.bfloat16)
    return mixed.reshape(mixed.shape[0], -1)


def body(
    tokens,
    segment_ids,
    first_gain,
    first_bias,
    query_key_value,
    project_out,
    second_gain,
    second_bias,
    up_weight,
    down_weight,
    final_gain,
    final_bias,
    merge_weight,
    owners,
):
    tok_rows = tokens.shape[0]
    width = tokens.shape[1]
    features = width * lax.axis_size("gx")
    qkv_full = lax.all_gather(query_key_value, "gy", axis=1, tiled=True)
    out_rows = lax.all_gather(project_out.T, "gy", axis=0, tiled=True)
    up_full = lax.all_gather(up_weight, "gy", axis=0, tiled=True)
    down_rows = lax.all_gather(down_weight.T, "gy", axis=0, tiled=True)
    merge_rows = lax.all_gather(
        merge_weight.transpose(2, 0, 1).reshape(merge_weight.shape[2], 4 * width),
        "gy",
        axis=0,
        tiled=True,
    )

    full_rows = side_by_side(line_call(None, tokens, True, 1, 0))
    normed = normalize_rows(full_rows, first_gain, first_bias).astype(jnp.bfloat16)
    qkv = jnp.einsum(
        "td,kdc->ktc", normed, qkv_full, preferred_element_type=jnp.float32
    ).astype(jnp.bfloat16)
    head_count = qkv.shape[2] // HEAD
    queries = qkv[0].reshape(tok_rows, head_count, HEAD)
    key_rows = qkv[1].reshape(tok_rows, head_count, HEAD)
    value_rows = qkv[2].reshape(tok_rows, head_count, HEAD)
    query_block = min(512, tok_rows)
    attended = jnp.concatenate(
        [
            attend(
                queries[at : at + query_block],
                segment_ids[at : at + query_block],
                key_rows,
                value_rows,
                segment_ids,
            )
            for at in range(0, tok_rows, query_block)
        ],
        axis=0,
    )
    resid_blocks = line_call(dest_terms(attended, out_rows, width), tokens, True, CHUNKS, 1)
    first_resid = lax.dynamic_index_in_dim(resid_blocks, lax.axis_index("gx"), 0, False)
    second_normed = normalize_rows(
        side_by_side(resid_blocks), second_gain, second_bias
    ).astype(jnp.bfloat16)
    upper = jnp.dot(second_normed, up_full, preferred_element_type=jnp.float32)
    hidden = jax.nn.gelu(upper, approximate=False).astype(jnp.bfloat16)
    second_resid = line_call(dest_terms(hidden, down_rows, width), first_resid, False, CHUNKS, 2)
    post_sums = lax.psum(row_sums(second_resid), "gx")
    final_normed = normalize_from_sums(
        second_resid,
        post_sums,
        features,
        own_slice(final_gain, width),
        own_slice(final_bias, width),
    ).astype(jnp.bfloat16)
    grouped = (
        final_normed.reshape(tok_rows // (2 * IMG_W), 2, IMG_W // 2, 2, width)
        .transpose(0, 2, 1, 3, 4)
        .reshape(tok_rows // 4, 4 * width)
    )
    projected = line_call(dest_terms(grouped, merge_rows, width), None, False, 2, 3)

    merged_rows = tok_rows // 4
    owner_count = lax.axis_size("gy")
    capacity = max(2, 2 * merged_rows // owner_count)
    owner_col = owners[:, 0]
    order = jnp.arange(merged_rows, dtype=jnp.int32)
    earlier = (owner_col[:, None] == owner_col[None, :]) & (order[None, :] < order[:, None])
    slot_rank = jnp.sum(earlier.astype(jnp.int32), axis=1)
    target = owner_col * capacity + slot_rank
    place = (
        jnp.arange(owner_count * capacity, dtype=jnp.int32)[:, None] == target[None, :]
    ).astype(jnp.bfloat16)
    outgoing = jnp.dot(place, projected, preferred_element_type=jnp.float32).astype(jnp.bfloat16)
    outgoing = outgoing.reshape(owner_count, capacity, width)
    arrived = lax.all_to_all(outgoing, "gy", split_axis=0, concat_axis=0, tiled=True)
    return arrived.reshape(1, owner_count, capacity, width)


def solution(mesh):
    in_specs = (
        P("gy", "gx"),
        P("gy"),
        P(),
        P(),
        P(None, "gy", "gx"),
        P("gx", "gy"),
        P(),
        P(),
        P("gy", "gx"),
        P("gx", "gy"),
        P(),
        P(),
        P(None, "gx", "gy"),
        P("gy", None),
    )
    out_specs = P("gy", None, None, "gx")
    return jax.shard_map(body, mesh=mesh, in_specs=in_specs, out_specs=out_specs, check_vma=False)
```
